32 devices in a mesh: chan: 16 (over z, y, x), tm: 2 (over core).
Axes of the slice: x: 2, y: 2, z: 4, core: 2. Of those that a mesh axis runs over, the one named last changes fastest.
Arguments:
- spectra: bfloat16 [2, 16, 10240, 2, 384], P('tm', 'chan'), as said below
- mask: int32 [2, 16, 10240], P('tm', 'chan'), may hold values from 0 to 1, as said below
Outputs:
- correlations: float32 [8, 10240, 3001], P('tm', 'chan')
The draws below stay inside these ranges and needn't reach their ends.
Inputs may be any that keep to these rules, and one draw needn't show every extreme that they name: `spectra`: spectra of the windows, of scales that vary over bins and over channels. `mask`: in every window, among the 640 channels of one block (channels b * 640 to (b + 1) * 640 - 1) at most 480 flags are 1.
All inputs are finite; a program needn't handle non-finite values.
Results may differ from the reference program's by a relative error of at most 0.004.
Values may be sent and summed in bfloat16 or wider, within the bound.
A program may use at most 320 MiB of HBM per device.

```python
import math
import jax
import jax.numpy as jnp
from jax import lax

CH = 10240
F = 384
F0 = 12
NFFT = 6000
MAXLAG = 1500
SB = 4
STEPS = 2
SRC = 8
LAGS = 3001
CH_DEV = 640
CAP = 480
WINS = 16
HALVES = 2


def draw_spectra(key, part):
    keys = jax.random.split(key, 3)
    shape = (HALVES, WINS, CH, 2, F)
    base = jax.random.normal(keys[0], shape, jnp.float32)
    column = jnp.exp(jax.random.uniform(keys[1], (F,), jnp.float32, 0.0, math.log(10.0)))
    row_scale = jnp.exp(jax.random.uniform(keys[2], (HALVES, WINS, CH, 1, 1), jnp.float32, 0.0, math.log(10.0)))
    return (base * column * row_scale).astype(jnp.bfloat16)


def draw_mask(key, part):
    keys = jax.random.split(key, 7)
    blocks = CH // CH_DEV
    windows = HALVES * WINS
    lanes = jnp.arange(CH_DEV, dtype=jnp.int32)
    dead_order = jax.random.randint(keys[0], (blocks, CH_DEV), 0, 65536) * CH_DEV + lanes
    dead_rank = jnp.argsort(jnp.argsort(dead_order, axis=1), axis=1)
    dead_count = jax.random.randint(keys[1], (blocks, 1), 0, CH_DEV - CAP + 1)
    dead = (dead_rank >= CH_DEV - dead_count).astype(jnp.int32)
    scores = jax.random.randint(keys[2], (windows, blocks, CH_DEV), 0, 65536) * CH_DEV + lanes + dead[None] * (65536 * CH_DEV)
    ranks = jnp.argsort(jnp.argsort(scores, axis=2), axis=2)
    floor_low = jax.random.randint(keys[3], (1, blocks), 1, CAP + 1)
    kept_count = jax.random.randint(keys[4], (windows, blocks), floor_low, CAP + 1)
    busiest = jax.random.randint(keys[5], (windows, 1), 0, blocks)
    fullest = jax.random.randint(keys[6], (1, 1), 0, blocks)
    block_index = jnp.arange(blocks, dtype=jnp.int32)[None, :]
    kept_count = jnp.where((block_index == busiest) | (block_index == fullest), CAP, kept_count)
    flags = (ranks < kept_count[..., None]).astype(jnp.int32)
    return flags.reshape(HALVES, WINS, CH)


def setup_inputs(seed: int = 0) -> dict:
    key_of = jax.random.split(jax.random.key(seed), 3)
    spectra = draw_spectra(jax.random.fold_in(key_of[2], 71), 0)
    mask = draw_mask(jax.random.fold_in(key_of[2], 71), 0)
    return {"spectra": spectra, "mask": mask}


def lag_table():
    bin_index = F0 + jnp.arange(F, dtype=jnp.int32)
    lag_index = jnp.arange(LAGS, dtype=jnp.int32) - MAXLAG
    phase_steps = jnp.mod(bin_index[:, None] * lag_index[None, :], NFFT)
    angles = phase_steps.astype(jnp.float32) * jnp.float32(2.0 * math.pi / NFFT)
    return jnp.concatenate([jnp.cos(angles), -jnp.sin(angles)], axis=0)

def whiten(window_spec, kept_mask):
    values = window_spec.astype(jnp.float32)
    energy = lax.optimization_barrier(jnp.sum(values * values, axis=(-2, -1))) / F
    factor = lax.rsqrt(energy + 1e-06) * kept_mask.astype(jnp.float32)
    return (values * factor[..., None, None]).astype(jnp.bfloat16)

def source_channels():
    which = jnp.arange(SRC, dtype=jnp.int32)
    return which // SB * (CH // CH_DEV // STEPS) * CH_DEV + which % SB

def reference(spectra, mask):
    chosen = source_channels()
    flat_spec = spectra.reshape(HALVES * WINS, CH, 2, F)
    flat_mask = mask.reshape(HALVES * WINS, CH)

    def add_window(totals, window):
        cross_sum, pair_count = totals
        window_spec, kept_mask = window
        whitened = whiten(window_spec, kept_mask).astype(jnp.float32)
        source_rows = whitened[chosen]
        source_keep = kept_mask[chosen].astype(jnp.float32)
        real_part = source_rows[:, None, 0] * whitened[None, :, 0] + source_rows[:, None, 1] * whitened[None, :, 1]
        imag_part = source_rows[:, None, 1] * whitened[None, :, 0] - source_rows[:, None, 0] * whitened[None, :, 1]
        cross_sum = cross_sum + jnp.stack([real_part, imag_part], axis=2)
        pair_count = pair_count + source_keep[:, None] * kept_mask.astype(jnp.float32)[None, :]
        return ((cross_sum, pair_count), None)
    start = (jnp.zeros((SRC, CH, 2, F), jnp.float32), jnp.zeros((SRC, CH), jnp.float32))
    (cross_sum, pair_count), _ = lax.scan(add_window, start, (flat_spec, flat_mask))
    lag_matrix = lag_table()

    def invert(pair_data):
        spectrum, counted = pair_data
        lagged = jnp.dot(spectrum.reshape(CH, 2 * F), lag_matrix, precision=lax.Precision.HIGHEST, preferred_element_type=jnp.float32)
        return lagged / jnp.maximum(counted, 1.0)[:, None]
    return lax.map(invert, (cross_sum, pair_count))
```

```python
import functools
import math

import jax
import jax.numpy as jnp
import numpy as np
from jax import lax
from jax.experimental import pallas as pl
from jax.experimental.pallas import tpu as pltpu
from jax.sharding import PartitionSpec as P

CH = 10240
F = 384
F0 = 12
NFFT = 6000
MAXLAG = 1500
SB = 4
STEPS = 2
SRC = SB * STEPS
LAGS = 3001
LANES = 128
TILE = 128
MESH = pl.DeviceIdType.MESH


def lag_table():
    bins = F0 + np.arange(F, dtype=np.int64)
    lags = np.arange(LAGS, dtype=np.int64) - MAXLAG
    angles = np.mod(lags[:, None] * bins[None, :], NFFT) * (2.0 * math.pi / NFFT)
    table = np.concatenate([np.cos(angles), -np.sin(angles)], axis=1)
    return jnp.asarray(table.astype(np.float32)).astype(jnp.bfloat16)


def whiten(values):
    energy = jnp.sum(values * values, axis=(-2, -1), keepdims=True) / F
    return values * lax.rsqrt(energy + 1e-06)


def offset(step, n):
    return n // 2 + (1 - 2 * (step % 2)) * ((step + 1) // 2)


def exchange_kernel(
    n, bw, capp, x_ref, aux_ref, src_ref, out_ref,
    xin, pk, rv, fw, aux_rv, aux_fw, acc, cnt,
    in_sem, send_sem, recv_sem, asend_sem, arecv_sem,
    fsend_sem, frecv_sem, afsend_sem, afrecv_sem,
):
    me = lax.axis_index("chan")
    tm = lax.axis_index("tm")
    other = 1 - tm
    chunks = -(-bw // LANES)

    barrier = pltpu.get_barrier_semaphore()

    def greet(k, _):
        pl.semaphore_signal(barrier, inc=1, device_id=((me + k) % n, tm), device_id_type=MESH)
        return 0

    lax.fori_loop(1, n, greet, 0)
    pl.semaphore_signal(barrier, inc=1, device_id=(me, other), device_id_type=MESH)
    pl.semaphore_wait(barrier, n)

    def dest(step):
        return (me + offset(step, n)) % n

    def load(step):
        rows = pl.ds(pl.multiple_of(dest(step) * bw, bw), bw)
        return pltpu.make_async_copy(
            x_ref.at[:, rows, :], xin.at[step % 2], in_sem.at[step % 2]
        )

    def pack(step):
        load(step).wait()
        slot = step % 2
        re = xin[slot, 0].astype(jnp.float32)
        im = xin[slot, 1].astype(jnp.float32)
        energy = jnp.sum(re * re + im * im, axis=1, keepdims=True) / F
        factor = lax.rsqrt(energy + 1e-06)
        re = (re * factor).astype(jnp.bfloat16)
        im = (im * factor).astype(jnp.bfloat16)
        place = lax.broadcasted_iota(jnp.int32, (capp, LANES), 0).astype(jnp.float32)
        pick = jnp.concatenate(
            [
                jnp.where(place == aux_ref[dest(step), i : i + 1, :], 1.0, 0.0).astype(jnp.bfloat16)
                for i in range(chunks)
            ],
            axis=1,
        )[:, :bw]
        pk[step, 0:capp, :] = jnp.dot(pick, re, preferred_element_type=jnp.float32).astype(jnp.bfloat16)
        pk[step, capp : 2 * capp, :] = jnp.dot(pick, im, preferred_element_type=jnp.float32).astype(jnp.bfloat16)
        pk[step, 2 * capp :, :] = src_ref[...]

    def main(step):
        to = (dest(step), tm)
        return (
            pltpu.make_async_remote_copy(
                src_ref=pk.at[step], dst_ref=rv.at[step], send_sem=send_sem.at[step],
                recv_sem=recv_sem.at[step], device_id=to, device_id_type=MESH,
            ),
            pltpu.make_async_remote_copy(
                src_ref=aux_ref.at[dest(step)], dst_ref=aux_rv.at[step], send_sem=asend_sem.at[step],
                recv_sem=arecv_sem.at[step], device_id=to, device_id_type=MESH,
            ),
        )

    def forward(step, rows, flags):
        to = (me, other)
        return (
            pltpu.make_async_remote_copy(
                src_ref=rows, dst_ref=fw.at[step], send_sem=fsend_sem.at[step],
                recv_sem=frecv_sem.at[step], device_id=to, device_id_type=MESH,
            ),
            pltpu.make_async_remote_copy(
                src_ref=flags, dst_ref=aux_fw.at[step], send_sem=afsend_sem.at[step],
                recv_sem=afrecv_sem.at[step], device_id=to, device_id_type=MESH,
            ),
        )

    load(0).start()

    def send(step, _):
        load(step + 1).start()
        pack(step)
        for copy in main(step):
            copy.start()
        return 0

    lax.fori_loop(0, n - 1, send, 0)
    last = n - 1
    pack(last)
    for copy in forward(last, pk.at[last], aux_ref.at[me]):
        copy.start()

    acc[...] = jnp.zeros_like(acc)
    cnt[...] = jnp.zeros_like(cnt)
    late = tm.astype(jnp.float32)

    def correlate(rows, flags):
        sources = rows[2 * capp :, :].astype(jnp.float32)
        a_re = sources[0:SB] * (1.0 - late) + sources[SB : 2 * SB] * late
        a_im = sources[2 * SB : 3 * SB] * (1.0 - late) + sources[3 * SB :] * late
        source_keep = flags[chunks : chunks + 1, :]
        diagonal = lax.broadcasted_iota(jnp.int32, (LANES, LANES), 0) == lax.broadcasted_iota(
            jnp.int32, (LANES, LANES), 1
        )
        place = lax.broadcasted_iota(jnp.int32, (LANES, capp), 1).astype(jnp.float32)
        for i in range(chunks):
            here = slice(i * LANES, (i + 1) * LANES)
            rank = jnp.sum(jnp.where(diagonal, flags[i : i + 1, :], 0.0), axis=1, keepdims=True)
            back = jnp.where(place == rank, 1.0, 0.0).astype(jnp.bfloat16)
            b_re = jnp.dot(back, rows[0:capp, :], preferred_element_type=jnp.float32)
            b_im = jnp.dot(back, rows[capp : 2 * capp, :], preferred_element_type=jnp.float32)
            for q in range(SB):
                acc[q, here, 0:F] += a_re[q : q + 1] * b_re + a_im[q : q + 1] * b_im
                acc[q, here, F : 2 * F] += a_im[q : q + 1] * b_re - a_re[q : q + 1] * b_im
            cnt[here, :] += jnp.where(rank >= 0.0, 1.0, 0.0) * source_keep

    correlate(pk.at[last], aux_ref.at[me])

    def wait_forward(step):
        for copy in forward(step, rv.at[step], aux_rv.at[step]):
            copy.wait_recv()
        correlate(fw.at[step], aux_fw.at[step])

    wait_forward(last)

    def receive(step, _):
        for copy in main(step):
            copy.wait_recv()
        for copy in forward(step, rv.at[step], aux_rv.at[step]):
            copy.start()
        correlate(rv.at[step], aux_rv.at[step])
        wait_forward(step)
        return 0

    lax.fori_loop(0, n - 1, receive, 0)

    lane = lax.broadcasted_iota(jnp.int32, (1, LANES), 1)
    for q in range(SB):
        mine = jnp.where(lane == tm * SB + q, 1.0, 0.0)
        counted = jnp.sum(cnt[...] * mine, axis=1, keepdims=True)
        out_ref[q] = (acc[q] * (1.0 / jnp.maximum(counted, 1.0))).astype(out_ref.dtype)

    def finish(step, _):
        for copy in main(step):
            copy.wait_send()
        for copy in forward(step, rv.at[step], aux_rv.at[step]):
            copy.wait_send()
        return 0

    lax.fori_loop(0, n - 1, finish, 0)
    for copy in forward(last, pk.at[last], aux_ref.at[me]):
        copy.wait_send()


def exchange(x, aux, src, n, bw, capp):
    chunks = -(-bw // LANES)
    bwp = chunks * LANES
    rows = 2 * capp + 2 * SRC
    block = pltpu.VMEM((n, rows, F), jnp.bfloat16)
    flags = pltpu.VMEM((n, 8, LANES), jnp.float32)
    sems = pltpu.SemaphoreType.DMA((n,))
    return pl.pallas_call(
        functools.partial(exchange_kernel, n, bw, capp),
        out_shape=jax.ShapeDtypeStruct((SB, bwp, 2 * F), jnp.bfloat16),
        in_specs=[
            pl.BlockSpec(memory_space=pl.ANY),
            pl.BlockSpec(memory_space=pltpu.VMEM),
            pl.BlockSpec(memory_space=pltpu.VMEM),
        ],
        out_specs=pl.BlockSpec(memory_space=pltpu.VMEM),
        scratch_shapes=[
            pltpu.VMEM((2, 2, bw, F), jnp.bfloat16),
            block, block, block, flags, flags,
            pltpu.VMEM((SB, bwp, 2 * F), jnp.float32),
            pltpu.VMEM((bwp, LANES), jnp.float32),
            pltpu.SemaphoreType.DMA((2,)),
        ] + [sems] * 8,
        compiler_params=pltpu.CompilerParams(
            collective_id=0, has_side_effects=True, vmem_limit_bytes=62 * 1024 * 1024
        ),
        name="exchange_correlate",
    )(x, aux, src)


def lags_kernel(bw, table_ref, cross_ref, out_ref, mixed):
    for q in range(SB):
        lagged = lax.dot_general(
            table_ref[...], cross_ref[q], (((1,), (1,)), ((), ())), preferred_element_type=jnp.float32
        )
        for i in range(mixed.shape[0]):
            mixed[i, pl.ds(q, TILE, stride=SB), :] = lagged[:, i * LANES : (i + 1) * LANES]
    for i in range(mixed.shape[0]):
        width = min(bw - i * LANES, LANES)
        block = mixed[i].reshape(TILE, SB, LANES)
        out_ref[:, :, i * LANES : i * LANES + width] = block[:, :, :width]


def to_lags(cross, table, bw):
    chunks = cross.shape[1] // LANES
    out = pl.pallas_call(
        functools.partial(lags_kernel, bw),
        grid=(-(-LAGS // TILE),),
        out_shape=jax.ShapeDtypeStruct((LAGS, SB, bw), jnp.float32),
        in_specs=[
            pl.BlockSpec((TILE, 2 * F), lambda t: (t, 0)),
            pl.BlockSpec((SB, chunks * LANES, 2 * F), lambda t: (0, 0, 0)),
        ],
        out_specs=pl.BlockSpec((TILE, SB, bw), lambda t: (t, 0, 0)),
        scratch_shapes=[pltpu.VMEM((chunks, TILE * SB, LANES), jnp.float32)],
        compiler_params=pltpu.CompilerParams(vmem_limit_bytes=48 * 1024 * 1024),
        name="to_lags",
    )(table, cross)
    return out.transpose(1, 2, 0)


def local(table, spectra, mask):
    n = lax.axis_size("chan")
    bw = CH // n
    cap = bw * 3 // 4
    capp = -(-cap // 16) * 16
    chunks = -(-bw // LANES)
    x = spectra[0, 0].transpose(1, 0, 2)
    keep = mask[0, 0].reshape(n, bw)
    upto = jnp.arange(bw)[:, None] <= jnp.arange(bw)[None, :]
    count = jnp.dot(
        keep.astype(jnp.bfloat16), upto.astype(jnp.bfloat16), preferred_element_type=jnp.float32
    )
    rank = jnp.where(keep > 0, count - 1.0, -1.0)
    rank = jnp.pad(rank, ((0, 0), (0, chunks * LANES - bw)), constant_values=-1.0)
    stride = n // STEPS
    source_keep = keep[::stride, :SB].reshape(1, 1, SRC).astype(jnp.float32)
    source_keep = jnp.broadcast_to(jnp.pad(source_keep, ((0, 0), (0, 0), (0, LANES - SRC))), (n, 1, LANES))
    aux = jnp.concatenate([rank.reshape(n, chunks, LANES), source_keep], axis=1)
    aux = jnp.pad(aux, ((0, 0), (0, 8 - chunks - 1), (0, 0)))
    first = spectra[0, 0].reshape(n, bw, 2, F)[::stride, :SB].reshape(SRC, 2, F)
    src = whiten(first.astype(jnp.float32)) * keep[::stride, :SB].reshape(SRC, 1, 1).astype(jnp.float32)
    src = src.astype(jnp.bfloat16).transpose(1, 0, 2).reshape(2 * SRC, F)
    cross = exchange(x, aux, src, n, bw, capp)
    return to_lags(cross, table, bw)


def solution(mesh):
    placed = (P("tm", "chan", None, None, None), P("tm", "chan", None))
    return jax.shard_map(
        functools.partial(local, lag_table()),
        mesh=mesh, in_specs=placed, out_specs=P("tm", "chan", None), check_vma=False,
    )
```

```python
import functools
import math

import jax
import jax.numpy as jnp
import numpy as np
from jax import lax
from jax.experimental import pallas as pl
from jax.experimental.pallas import tpu as pltpu
from jax.sharding import PartitionSpec as P

CH = 10240
F = 384
F0 = 12
NFFT = 6000
MAXLAG = 1500
SB = 4
STEPS = 2
SRC = SB * STEPS
LAGS = 3001
LANES = 128
AHEAD = 6
TILE = 512
MESH = pl.DeviceIdType.MESH


def lag_table():
    bins = F0 + np.arange(F, dtype=np.int64)
    lags = np.arange(LAGS, dtype=np.int64) - MAXLAG
    angles = np.mod(lags[:, None] * bins[None, :], NFFT) * (2.0 * math.pi / NFFT)
    table = np.concatenate([np.cos(angles), -np.sin(angles)], axis=1)
    return jnp.asarray(table.astype(np.float32)).astype(jnp.bfloat16)


def whiten(values):
    energy = jnp.sum(values * values, axis=(-2, -1), keepdims=True) / F
    return values * lax.rsqrt(energy + 1e-06)


def partner(me, step, n):
    k = step % 2 * ((step + 1) // 2 % (n // 2)) + (1 - step % 2) * (n // 2 + step // 2)
    place, bit = 0, 1
    while bit < n:
        place += (me // bit + k // bit) % 2 * bit
        bit *= 2
    return place


def exchange_kernel(
    n, bw, capp, x_ref, aux_ref, src_ref, out_ref,
    xin, pk, rv, fw, aux_rv, aux_fw, acc, cnt,
    in_sem, send_sem, recv_sem, asend_sem, arecv_sem,
    fsend_sem, frecv_sem, afsend_sem, afrecv_sem,
):
    me = lax.axis_index("chan")
    tm = lax.axis_index("tm")
    other = 1 - tm
    chunks = -(-bw // LANES)

    barrier = pltpu.get_barrier_semaphore()

    def greet(k, _):
        pl.semaphore_signal(barrier, inc=1, device_id=((me + k) % n, tm), device_id_type=MESH)
        return 0

    lax.fori_loop(1, n, greet, 0)
    pl.semaphore_signal(barrier, inc=1, device_id=(me, other), device_id_type=MESH)
    pl.semaphore_wait(barrier, n)

    def dest(step):
        return partner(me, step, n)

    def load(step):
        rows = pl.ds(pl.multiple_of(dest(step) * bw, bw), bw)
        return pltpu.make_async_copy(
            x_ref.at[:, rows, :], xin.at[step % 2], in_sem.at[step % 2]
        )

    def pack(step):
        load(step).wait()
        slot = step % 2
        re = xin[slot, 0].astype(jnp.float32)
        im = xin[slot, 1].astype(jnp.float32)
        energy = jnp.sum(re * re + im * im, axis=1, keepdims=True) / F
        factor = lax.rsqrt(energy + 1e-06)
        re = (re * factor).astype(jnp.bfloat16)
        im = (im * factor).astype(jnp.bfloat16)
        place = lax.broadcasted_iota(jnp.int32, (capp, LANES), 0).astype(jnp.float32)
        pick = jnp.concatenate(
            [
                jnp.where(place == aux_ref[dest(step), i : i + 1, :], 1.0, 0.0).astype(jnp.bfloat16)
                for i in range(chunks)
            ],
            axis=1,
        )[:, :bw]
        pk[step, 0:capp, :] = jnp.dot(pick, re, preferred_element_type=jnp.float32).astype(jnp.bfloat16)
        pk[step, capp : 2 * capp, :] = jnp.dot(pick, im, preferred_element_type=jnp.float32).astype(jnp.bfloat16)
        pk[step, 2 * capp :, :] = src_ref[...]

    def main(step):
        to = (dest(step), tm)
        return (
            pltpu.make_async_remote_copy(
                src_ref=pk.at[step], dst_ref=rv.at[step], send_sem=send_sem.at[step],
                recv_sem=recv_sem.at[step], device_id=to, device_id_type=MESH,
            ),
            pltpu.make_async_remote_copy(
                src_ref=aux_ref.at[dest(step)], dst_ref=aux_rv.at[step], send_sem=asend_sem.at[step],
                recv_sem=arecv_sem.at[step], device_id=to, device_id_type=MESH,
            ),
        )

    def forward(step, rows, flags):
        to = (me, other)
        return (
            pltpu.make_async_remote_copy(
                src_ref=rows, dst_ref=fw.at[step], send_sem=fsend_sem.at[step],
                recv_sem=frecv_sem.at[step], device_id=to, device_id_type=MESH,
            ),
            pltpu.make_async_remote_copy(
                src_ref=flags, dst_ref=aux_fw.at[step], send_sem=afsend_sem.at[step],
                recv_sem=afrecv_sem.at[step], device_id=to, device_id_type=MESH,
            ),
        )

    load(0).start()

    def send(step, _):
        load(step + 1).start()
        pack(step)
        for copy in main(step):
            copy.start()
        return 0

    def prepare(step, _):
        load(step + 1).start()
        pack(step)
        return 0

    last = n - 1
    lax.fori_loop(0, AHEAD, send, 0)
    lax.fori_loop(AHEAD, last, prepare, 0)
    pack(last)
    for copy in forward(last, pk.at[last], aux_ref.at[me]):
        copy.start()

    acc[...] = jnp.zeros_like(acc)
    cnt[...] = jnp.zeros_like(cnt)
    late = tm.astype(jnp.float32)

    def correlate(rows, flags):
        sources = rows[2 * capp :, :].astype(jnp.float32)
        a_re = sources[0:SB] * (1.0 - late) + sources[SB : 2 * SB] * late
        a_im = sources[2 * SB : 3 * SB] * (1.0 - late) + sources[3 * SB :] * late
        source_keep = flags[chunks : chunks + 1, :]
        diagonal = lax.broadcasted_iota(jnp.int32, (LANES, LANES), 0) == lax.broadcasted_iota(
            jnp.int32, (LANES, LANES), 1
        )
        place = lax.broadcasted_iota(jnp.int32, (LANES, capp), 1).astype(jnp.float32)
        for i in range(chunks):
            here = slice(i * LANES, (i + 1) * LANES)
            rank = jnp.sum(jnp.where(diagonal, flags[i : i + 1, :], 0.0), axis=1, keepdims=True)
            back = jnp.where(place == rank, 1.0, 0.0).astype(jnp.bfloat16)
            b_re = jnp.dot(back, rows[0:capp, :], preferred_element_type=jnp.float32)
            b_im = jnp.dot(back, rows[capp : 2 * capp, :], preferred_element_type=jnp.float32)
            for q in range(SB):
                acc[q, here, 0:F] += a_re[q : q + 1] * b_re + a_im[q : q + 1] * b_im
                acc[q, here, F : 2 * F] += a_im[q : q + 1] * b_re - a_re[q : q + 1] * b_im
            cnt[here, :] += jnp.where(rank >= 0.0, 1.0, 0.0) * source_keep

    correlate(pk.at[last], aux_ref.at[me])

    def wait_forward(step):
        for copy in forward(step, rv.at[step], aux_rv.at[step]):
            copy.wait_recv()
        correlate(fw.at[step], aux_fw.at[step])

    def receive(step, _):
        for copy in main(step):
            copy.wait_recv()
        for copy in forward(step, rv.at[step], aux_rv.at[step]):
            copy.start()

        @pl.when(step + AHEAD < last)
        def _():
            for copy in main(step + AHEAD):
                copy.start()

        correlate(rv.at[step], aux_rv.at[step])
        wait_forward((step + last) % n)
        return 0

    lax.fori_loop(0, last, receive, 0)
    wait_forward(last - 1)

    lane = lax.broadcasted_iota(jnp.int32, (1, LANES), 1)
    for q in range(SB):
        mine = jnp.where(lane == tm * SB + q, 1.0, 0.0)
        counted = jnp.sum(cnt[...] * mine, axis=1, keepdims=True)
        out_ref[q] = (acc[q] * (1.0 / jnp.maximum(counted, 1.0))).astype(out_ref.dtype)

    def finish(step, _):
        for copy in main(step):
            copy.wait_send()
        for copy in forward(step, rv.at[step], aux_rv.at[step]):
            copy.wait_send()
        return 0

    lax.fori_loop(0, n - 1, finish, 0)
    for copy in forward(last, pk.at[last], aux_ref.at[me]):
        copy.wait_send()


def exchange(x, aux, src, n, bw, capp):
    chunks = -(-bw // LANES)
    bwp = chunks * LANES
    rows = 2 * capp + 2 * SRC
    block = pltpu.VMEM((n, rows, F), jnp.bfloat16)
    flags = pltpu.VMEM((n, 8, LANES), jnp.float32)
    sems = pltpu.SemaphoreType.DMA((n,))
    return pl.pallas_call(
        functools.partial(exchange_kernel, n, bw, capp),
        out_shape=jax.ShapeDtypeStruct((SB, bwp, 2 * F), jnp.bfloat16),
        in_specs=[
            pl.BlockSpec(memory_space=pl.ANY),
            pl.BlockSpec(memory_space=pltpu.VMEM),
            pl.BlockSpec(memory_space=pltpu.VMEM),
        ],
        out_specs=pl.BlockSpec(memory_space=pltpu.VMEM),
        scratch_shapes=[
            pltpu.VMEM((2, 2, bw, F), jnp.bfloat16),
            block, block, block, flags, flags,
            pltpu.VMEM((SB, bwp, 2 * F), jnp.float32),
            pltpu.VMEM((bwp, LANES), jnp.float32),
            pltpu.SemaphoreType.DMA((2,)),
        ] + [sems] * 8,
        compiler_params=pltpu.CompilerParams(
            collective_id=0, has_side_effects=True, vmem_limit_bytes=62 * 1024 * 1024
        ),
        name="exchange_correlate",
    )(x, aux, src)


def lags_kernel(bw, table_ref, cross_ref, out_ref, mixed):
    for q in range(SB):
        lagged = lax.dot_general(
            table_ref[...], cross_ref[q], (((1,), (1,)), ((), ())), preferred_element_type=jnp.float32
        )
        for i in range(mixed.shape[0]):
            mixed[i, pl.ds(q, TILE, stride=SB), :] = lagged[:, i * LANES : (i + 1) * LANES]
    for i in range(mixed.shape[0]):
        width = min(bw - i * LANES, LANES)
        block = mixed[i].reshape(TILE, SB, LANES)
        out_ref[:, :, i * LANES : i * LANES + width] = block[:, :, :width]


def to_lags(cross, table, bw):
    chunks = cross.shape[1] // LANES
    out = pl.pallas_call(
        functools.partial(lags_kernel, bw),
        grid=(-(-LAGS // TILE),),
        out_shape=jax.ShapeDtypeStruct((LAGS, SB, bw), jnp.float32),
        in_specs=[
            pl.BlockSpec((TILE, 2 * F), lambda t: (t, 0)),
            pl.BlockSpec((SB, chunks * LANES, 2 * F), lambda t: (0, 0, 0)),
        ],
        out_specs=pl.BlockSpec((TILE, SB, bw), lambda t: (t, 0, 0)),
        scratch_shapes=[pltpu.VMEM((chunks, TILE * SB, LANES), jnp.float32)],
        compiler_params=pltpu.CompilerParams(vmem_limit_bytes=48 * 1024 * 1024),
        name="to_lags",
    )(table, cross)
    return out.transpose(1, 2, 0)


def local(table, spectra, mask):
    n = lax.axis_size("chan")
    bw = CH // n
    cap = bw * 3 // 4
    capp = -(-cap // 16) * 16
    chunks = -(-bw // LANES)
    x = spectra[0, 0].transpose(1, 0, 2)
    keep = mask[0, 0].reshape(n, bw)
    upto = jnp.arange(bw)[:, None] <= jnp.arange(bw)[None, :]
    count = jnp.dot(
        keep.astype(jnp.bfloat16), upto.astype(jnp.bfloat16), preferred_element_type=jnp.float32
    )
    rank = jnp.where(keep > 0, count - 1.0, -1.0)
    rank = jnp.pad(rank, ((0, 0), (0, chunks * LANES - bw)), constant_values=-1.0)
    stride = n // STEPS
    source_keep = keep[::stride, :SB].reshape(1, 1, SRC).astype(jnp.float32)
    source_keep = jnp.broadcast_to(jnp.pad(source_keep, ((0, 0), (0, 0), (0, LANES - SRC))), (n, 1, LANES))
    aux = jnp.concatenate([rank.reshape(n, chunks, LANES), source_keep], axis=1)
    aux = jnp.pad(aux, ((0, 0), (0, 8 - chunks - 1), (0, 0)))
    first = spectra[0, 0].reshape(n, bw, 2, F)[::stride, :SB].reshape(SRC, 2, F)
    src = whiten(first.astype(jnp.float32)) * keep[::stride, :SB].reshape(SRC, 1, 1).astype(jnp.float32)
    src = src.astype(jnp.bfloat16).transpose(1, 0, 2).reshape(2 * SRC, F)
    cross = exchange(x, aux, src, n, bw, capp)
    return to_lags(cross, table, bw)


def solution(mesh):
    placed = (P("tm", "chan", None, None, None), P("tm", "chan", None))
    return jax.shard_map(
        functools.partial(local, lag_table()),
        mesh=mesh, in_specs=placed, out_specs=P("tm", "chan", None), check_vma=False,
    )
```
